256 devices in a mesh: dp: 16 (over x, y_lo, core), prec: 8 (over z), pair: 2 (over y_hi).
Axes of the slice: x: 4, y: 4 (y_hi: 2, y_lo: 2; y = y_hi * 2 + y_lo), z: 8, core: 2. Of those that a mesh axis runs over, the one named last changes fastest.
Arguments:
- activations: bfloat16 [4096, 4096], P('dp', 'prec')
- output_grads: bfloat16 [4096, 16384], P('dp', 'pair')
- iter_counts: int32 [32, 8], P(('pair', 'dp'), 'prec'), may hold values from 1 to 2, as said below
Outputs:
- preconditioned: float32 [16384, 4096], P(('pair', 'dp'), 'prec')
The draws below stay inside these ranges and needn't reach their ends.
Inputs may be any that keep to these rules, and one draw needn't show every extreme that they name: `iter_counts`: newton iterations of each block; 2 is taken by at least one block in every draw.
All inputs are finite; a program needn't handle non-finite values.
Results may differ from the reference program's by a relative error of at most 0.0003.
Values may be sent and summed in bfloat16 or wider, within the bound.
No kernel may reach another device: no remote copies, remote signals or barrier semaphores. Data moves between devices by JAX's collectives and lax.ppermute only.
A program may use at most 64 MiB of HBM per device.

```python
import math
import jax
import jax.numpy as jnp
from jax import lax

D = 4096
FF = 16384
BLK = 512
ITERS = 2
TOKENS = 4096


def feature_scales(key, width):
    jitter = jnp.exp(jax.random.uniform(key, (width,), minval=0.0, maxval=math.log(10.0)))
    incline = jnp.exp(jnp.arange(width, dtype=jnp.float32) * (math.log(3.0) / width))
    return jitter * incline / 8.9


def scaled_values(key, rows_total, width, spread):
    first, second = jax.random.split(key, 2)
    scales = feature_scales(first, width) * spread
    values = jax.random.normal(second, (rows_total, width)) * scales
    return values


def draw_activations(key, part):
    key = jax.random.fold_in(key, 1)
    return scaled_values(key, TOKENS, D, 1.0).astype(jnp.bfloat16)


def draw_output_grads(key, part):
    key = jax.random.fold_in(key, 2)
    return scaled_values(key, TOKENS, FF, 1.0 / math.sqrt(TOKENS)).astype(jnp.bfloat16)


def draw_iter_counts(key, part):
    key = jax.random.fold_in(key, 3)
    first, second = jax.random.split(key)
    shape = (FF // BLK, D // BLK)
    lottery = jax.random.randint(first, shape, 0, 16)
    plan = jnp.where(lottery == 0, ITERS, 1)
    chosen = jax.random.randint(second, (), 0, shape[0] * shape[1])
    places = jnp.arange(shape[0] * shape[1], dtype=jnp.int32).reshape(shape)
    return jnp.where(places == chosen, ITERS, plan).astype(jnp.int32)


def setup_inputs(seed: int = 0) -> dict:
    streams_of = jax.random.split(jax.random.key(seed), 4)
    activations = draw_activations(jax.random.fold_in(streams_of[3], 71), 0)
    output_grads = draw_output_grads(jax.random.fold_in(streams_of[3], 71), 0)
    iter_counts = draw_iter_counts(jax.random.fold_in(streams_of[3], 71), 0)
    return dict(activations=activations, output_grads=output_grads, iter_counts=iter_counts)


SHIFT = 0.001

def product(left, right):
    return jnp.dot(left, right, precision=lax.Precision.HIGHEST)

def inverse_root(statistic, plan):
    extent = statistic.shape[0]
    identity = jnp.eye(extent, dtype=statistic.dtype)
    shifted = statistic + SHIFT * identity
    scaling = 2.5 / jnp.sqrt(jnp.sum(shifted * shifted) + 1e-06)
    inverse = identity * jnp.sqrt(jnp.sqrt(scaling))
    coupled = shifted * scaling

    def advance(step_index, state_pair):
        current, matrix = state_pair
        factor = 1.25 * identity - 0.25 * matrix
        square = product(factor, factor)
        return (product(current, factor), product(product(square, square), matrix))
    inverse, coupled = lax.fori_loop(0, plan, advance, (inverse, coupled))
    return inverse

def precondition(block, plan):
    left_root = inverse_root(product(block, block.T), plan)
    right_root = inverse_root(product(block.T, block), plan)
    return product(product(left_root, block), right_root)

def reference(activations, output_grads, iter_counts):
    grad = jnp.dot(output_grads.T, activations, preferred_element_type=jnp.float32)
    ff_blocks = FF // BLK
    d_blocks = D // BLK
    blocks = grad.reshape(ff_blocks, BLK, d_blocks, BLK).transpose(0, 2, 1, 3).reshape(ff_blocks * d_blocks, BLK, BLK)
    updates = lax.map(lambda item: precondition(item[0], item[1]), (blocks, iter_counts.reshape(-1)))
    graft_ratio = jnp.sqrt(jnp.sum(grad * grad) / jnp.sum(updates * updates))
    scaled = updates * graft_ratio
    return scaled.reshape(ff_blocks, d_blocks, BLK, BLK).transpose(0, 2, 1, 3).reshape(FF, D)
```

```python
import jax
import jax.numpy as jnp
from jax import lax
from jax.experimental import pallas as pl
from jax.experimental.pallas import tpu as pltpu
from jax.sharding import Mesh, PartitionSpec as P

BLK = 512
SHIFT = 0.001
DP = ("x", "yl", "core")
EVERY = ("x", "yl", "core", "prec", "pair")
ROWS_BY_ROWS = (((1,), (1,)), ((), ()))
ROWS_BY_COLUMNS = (((1,), (0,)), ((), ()))


def dot(left, right, contract=ROWS_BY_COLUMNS):
    return lax.dot_general(left, right, contract, preferred_element_type=jnp.float32)


def split(matrix):
    high = matrix.astype(jnp.bfloat16)
    return high, (matrix - high.astype(jnp.float32)).astype(jnp.bfloat16)


def product(left, right, contract=ROWS_BY_COLUMNS):
    (left_high, left_low), (right_high, right_low) = left, right
    return dot(left_high, right_high, contract) + (
        dot(left_high, right_low, contract) + dot(left_low, right_high, contract)
    )


def block_step(place_ref, grads_ref, near_ref, far_ref, update_ref, sums_ref, grad_ref, root_ref):
    shard = place_ref[0, 1]
    total = None
    for part in range(16):
        across, step = part // 8, part % 8
        offset = (step % 4) * 4 + (step // 4) * 2 + across
        acts_ref = far_ref if across else near_ref
        term = dot(acts_ref[step], grads_ref[shard ^ offset])
        total = term if total is None else total + term
    grad_ref[...] = total
    grad = grad_ref[...]
    grad_parts = split(grad)
    statistic = product(grad_parts, grad_parts, ROWS_BY_ROWS)
    on_diagonal = lax.broadcasted_iota(jnp.int32, (BLK, BLK), 0) == lax.broadcasted_iota(
        jnp.int32, (BLK, BLK), 1
    )
    shifted = statistic + jnp.where(on_diagonal, jnp.float32(SHIFT), jnp.float32(0.0))
    scaling = 2.5 / jnp.sqrt(jnp.sum(shifted * shifted) + 1e-06)
    root_ref[...] = jnp.where(on_diagonal, jnp.float32(1.25), jnp.float32(0.0)) - (
        0.25 * scaling
    ) * shifted

    @pl.when(place_ref[0, 0] == 2)
    def _():
        factor = root_ref[...]
        factor_parts = split(factor)
        square = product(factor_parts, factor_parts)
        square_parts = split(square)
        fourth = product(square_parts, square_parts)
        root_ref[...] = 1.25 * factor + product(split(fourth), split(square - 1.25 * factor))

    root_parts = split(root_ref[...])
    half = product(root_parts, grad_parts)
    update = product(root_parts, split(half)) * jnp.sqrt(scaling)
    update_ref[...] = update.T
    lane = lax.broadcasted_iota(jnp.int32, (8, 128), 1)
    grad_squares = jnp.sum(grad * grad)
    update_squares = jnp.sum(update * update)
    sums_ref[...] = jnp.where(lane == 0, grad_squares, jnp.where(lane == 1, update_squares, 0.0))


def run_block(place, grads, near, far):
    vmem = pl.BlockSpec(memory_space=pltpu.VMEM)
    return pl.pallas_call(
        block_step,
        out_shape=(
            jax.ShapeDtypeStruct((BLK, BLK), jnp.float32),
            jax.ShapeDtypeStruct((8, 128), jnp.float32),
        ),
        in_specs=[pl.BlockSpec(memory_space=pltpu.SMEM), vmem, vmem, vmem],
        out_specs=(vmem, vmem),
        scratch_shapes=[pltpu.VMEM((BLK, BLK), jnp.float32)] * 2,
        compiler_params=pltpu.CompilerParams(vmem_limit_bytes=48 << 20),
    )(place, grads, near, far)


def swap(value, axes, bits):
    size = 1
    for axis in axes:
        size *= lax.axis_size(axis)
    return lax.ppermute(value, axes, [(i, i ^ bits) for i in range(size)])


def per_device(activations, output_grads, iter_counts):
    tokens = output_grads.shape[0]
    shards = 16
    pieces = output_grads.reshape(tokens, shards, BLK).transpose(1, 0, 2)
    grads = lax.all_to_all(pieces, DP, 0, 0, tiled=True)

    own = activations.T
    along_x = jnp.stack([own] + [swap(own, ("x",), bits) for bits in (1, 2, 3)])
    near = jnp.concatenate([along_x, swap(along_x, ("yl", "pair"), 3)])
    far = swap(near, ("core",), 1)

    place = jnp.stack([iter_counts[0, 0], lax.axis_index(DP)]).reshape(1, 2).astype(jnp.int32)
    update, sums = run_block(place, grads, near, far)

    shared = jnp.broadcast_to(sums[None, :1], (256, 1, 128))
    gathered = lax.all_to_all(shared, EVERY, 0, 0, tiled=True)
    totals = jnp.sum(gathered, axis=(0, 1))
    return update * jnp.sqrt(totals[0] / totals[1])


def solution(mesh):
    fine = Mesh(mesh.devices.reshape(4, 2, 2, 8, 2), EVERY)
    in_specs = (P(DP, "prec"), P(DP, "pair"), P(("pair",) + DP, "prec"))
    out_specs = P(("pair",) + DP, "prec")
    return jax.shard_map(
        per_device, mesh=fine, in_specs=in_specs, out_specs=out_specs, check_vma=False
    )
```

```python
import jax
import jax.numpy as jnp
from jax import lax
from jax.experimental import pallas as pl
from jax.experimental.pallas import tpu as pltpu
from jax.sharding import Mesh, PartitionSpec as P

BLK = 512
SHIFT = 0.001
DP = ("x", "yl", "core")
EVERY = ("x", "yl", "core", "prec", "pair")
ROWS_BY_ROWS = (((1,), (1,)), ((), ()))
ROWS_BY_COLUMNS = (((1,), (0,)), ((), ()))
CUT_LIMIT = 48 << 20
HALF_LIMIT = 24 << 20
VMEM_LIMIT = 24 << 20
GRAFT_LIMIT = 8 << 20
HALF = 128
GROUPS = tuple(
    tuple(4 * x + offset for x in some) for offset in (0, 2, 1, 3) for some in ((0, 1, 3), (2,))
)


def dot(left, right, contract=ROWS_BY_COLUMNS):
    return lax.dot_general(left, right, contract, preferred_element_type=jnp.float32)


def split(matrix):
    high = matrix.astype(jnp.bfloat16)
    return high, (matrix - high.astype(jnp.float32)).astype(jnp.bfloat16)


def product(left, right, contract=ROWS_BY_COLUMNS):
    (left_high, left_low), (right_high, right_low) = left, right
    return dot(left_high, right_high, contract) + (
        dot(left_high, right_low, contract) + dot(left_low, right_high, contract)
    )


def cut_step(place_ref, grads_ref, out_ref, sems):
    first = pl.multiple_of(place_ref[0, 2] * HALF, HALF)
    copies = []
    for shard in range(out_ref.shape[0]):
        source = grads_ref.at[pl.ds(first, HALF), pl.ds(shard * BLK, BLK)]
        copies.append(pltpu.make_async_copy(source, out_ref.at[shard], sems.at[shard]))
    for copy in copies:
        copy.start()
    for copy in copies:
        copy.wait()


def cut(place, grads):
    shards = grads.shape[1] // BLK
    return pl.pallas_call(
        cut_step,
        out_shape=jax.ShapeDtypeStruct((shards, HALF, BLK), grads.dtype),
        in_specs=[pl.BlockSpec(memory_space=pltpu.SMEM), pl.BlockSpec(memory_space=pl.ANY)],
        out_specs=pl.BlockSpec(memory_space=pltpu.VMEM),
        scratch_shapes=[pltpu.SemaphoreType.DMA((shards,))],
        compiler_params=pltpu.CompilerParams(vmem_limit_bytes=CUT_LIMIT),
    )(place, grads)


def half_step(place_ref, mine_ref, *refs):
    acts, (partial_ref, rest_ref, acts_ref) = refs[:-3], refs[-3:]
    shard, odd = place_ref[0, 1], place_ref[0, 2]
    mine = pl.ds(pl.multiple_of(odd * HALF, HALF), HALF)
    theirs = pl.ds(pl.multiple_of((1 - odd) * HALF, HALF), HALF)
    for group, group_ref in enumerate(acts):
        for slot, bits in enumerate(GROUPS[group]):
            columns = pl.ds(pl.multiple_of((shard ^ bits) * HALF, HALF), HALF)
            acts_ref[:, columns] = group_ref[slot, :, mine]
            rest_ref[:, columns] = group_ref[slot, :, theirs]
    shards = mine_ref.shape[0]
    partial_ref[...] = dot(acts_ref[...], mine_ref[...].reshape(shards * HALF, BLK))


def half_gradient(place, mine, acts):
    vmem = pl.BlockSpec(memory_space=pltpu.VMEM)
    tokens = mine.shape[0] * HALF
    return pl.pallas_call(
        half_step,
        out_shape=(
            jax.ShapeDtypeStruct((BLK, BLK), jnp.float32),
            jax.ShapeDtypeStruct((BLK, tokens), mine.dtype),
        ),
        in_specs=[pl.BlockSpec(memory_space=pltpu.SMEM)] + [vmem] * (1 + len(acts)),
        out_specs=(vmem, vmem),
        scratch_shapes=[pltpu.VMEM((BLK, tokens), mine.dtype)],
        compiler_params=pltpu.CompilerParams(vmem_limit_bytes=HALF_LIMIT),
    )(place, mine, *acts)


def block_step(place_ref, partial_ref, rest_ref, first_ref, second_ref, update_ref, sums_ref, root_ref):
    some = rest_ref.shape[1] // 2
    transposed = (
        partial_ref[...]
        + dot(rest_ref[:, :some], first_ref[...].reshape(some, BLK))
        + dot(rest_ref[:, some:], second_ref[...].reshape(some, BLK))
    )
    parts = split(transposed)
    statistic = product(parts, parts, ROWS_BY_ROWS)
    grad_parts = split(transposed.T)
    on_diagonal = lax.broadcasted_iota(jnp.int32, (BLK, BLK), 0) == lax.broadcasted_iota(
        jnp.int32, (BLK, BLK), 1
    )
    shifted = statistic + jnp.where(on_diagonal, jnp.float32(SHIFT), jnp.float32(0.0))
    scaling = 2.5 / jnp.sqrt(jnp.sum(shifted * shifted) + 1e-06)
    root_ref[...] = jnp.where(on_diagonal, jnp.float32(1.25), jnp.float32(0.0)) - (
        0.25 * scaling
    ) * shifted

    @pl.when(place_ref[0, 0] == 2)
    def _():
        factor = root_ref[...]
        factor_parts = split(factor)
        square = product(factor_parts, factor_parts)
        square_parts = split(square)
        fourth = product(square_parts, square_parts)
        root_ref[...] = 1.25 * factor + product(split(fourth), split(square - 1.25 * factor))

    root_parts = split(root_ref[...])
    half = product(grad_parts, root_parts)
    update = product(split(half), root_parts) * jnp.sqrt(scaling)
    update_ref[...] = update
    lane = lax.broadcasted_iota(jnp.int32, sums_ref.shape, 2)
    grad_squares = jnp.sum(transposed * transposed)
    update_squares = jnp.sum(update * update)
    sums_ref[...] = jnp.where(lane == 0, grad_squares, jnp.where(lane == 1, update_squares, 0.0))


def run_block(place, partial, rest, first, second, devices):
    vmem = pl.BlockSpec(memory_space=pltpu.VMEM)
    return pl.pallas_call(
        block_step,
        out_shape=(
            jax.ShapeDtypeStruct((BLK, BLK), jnp.float32),
            jax.ShapeDtypeStruct((devices, 1, 128), jnp.float32),
        ),
        in_specs=[pl.BlockSpec(memory_space=pltpu.SMEM)] + [vmem] * 4,
        out_specs=(vmem, vmem),
        scratch_shapes=[pltpu.VMEM((BLK, BLK), jnp.float32)],
        compiler_params=pltpu.CompilerParams(vmem_limit_bytes=VMEM_LIMIT),
    )(place, partial, rest, first, second)


def graft_step(sums_ref, update_ref, out_ref):
    totals = jnp.sum(sums_ref[...], axis=0)
    lane = lax.broadcasted_iota(jnp.int32, totals.shape, 1)
    grad_squares = jnp.sum(jnp.where(lane == 0, totals, 0.0))
    update_squares = jnp.sum(jnp.where(lane == 1, totals, 0.0))
    out_ref[...] = update_ref[...] * jnp.sqrt(grad_squares / update_squares)


def graft(sums, update):
    vmem = pl.BlockSpec(memory_space=pltpu.VMEM)
    return pl.pallas_call(
        graft_step,
        out_shape=jax.ShapeDtypeStruct(update.shape, update.dtype),
        in_specs=[vmem, vmem],
        out_specs=vmem,
        compiler_params=pltpu.CompilerParams(vmem_limit_bytes=GRAFT_LIMIT),
    )(sums, update)


def swap(value, axes, bits):
    size = 1
    for axis in axes:
        size *= lax.axis_size(axis)
    return lax.ppermute(value, axes, [(i, i ^ bits) for i in range(size)])


def swap_planes(value, up):
    step = 1 if up else -1
    pairs = [(i, (i + (step if i % 2 == 0 else -step)) % 8) for i in range(8)]
    return lax.ppermute(value, "prec", pairs)


def per_device(activations, output_grads, iter_counts):
    odd = lax.axis_index("prec") % 2
    place = jnp.stack([iter_counts[0, 0], lax.axis_index(DP), odd]).reshape(1, 3).astype(jnp.int32)
    own = activations.T
    near = [swap(own, ("x",), bits) for bits in (1, 3)]
    mine = cut(place, output_grads)
    three = jnp.stack([own] + near)
    mine, three = lax.optimization_barrier((mine, three))
    mine = lax.all_to_all(mine, DP, 0, 0, tiled=True)
    last = swap(three[1:2], ("x",), 3)
    acts = [three, last] + [swap(value, ("yl", "pair"), 3) for value in (three, last)]
    acts += [swap(value, ("core",), 1) for value in acts]
    half = mine.shape[0] // 2
    first, second = swap_planes(mine[:half], True), swap_planes(mine[half:], False)
    partial, rest = half_gradient(place, mine, acts)

    devices = 256
    update, sums = run_block(place, partial, rest, first, second, devices)
    sums = lax.all_to_all(sums, EVERY, 0, 0, tiled=True)
    return graft(sums, update)


def solution(mesh):
    fine = Mesh(mesh.devices.reshape(4, 2, 2, 8, 2), EVERY)
    in_specs = (P(DP, "prec"), P(DP, "pair"), P(("pair",) + DP, "prec"))
    out_specs = P(("pair",) + DP, "prec")
    return jax.shard_map(
        per_device, mesh=fine, in_specs=in_specs, out_specs=out_specs, check_vma=False
    )
```

```python
import jax
import jax.numpy as jnp
from jax import lax
from jax.experimental import pallas as pl
from jax.experimental.pallas import tpu as pltpu
from jax.sharding import Mesh, PartitionSpec as P

BLK = 512
SHIFT = 0.001
DP = ("x", "yl", "core")
EVERY = ("x", "yl", "core", "prec", "pair")
ROWS_BY_ROWS = (((1,), (1,)), ((), ()))
ROWS_BY_COLUMNS = (((1,), (0,)), ((), ()))
CUT_LIMIT = 48 << 20
HALF_LIMIT = 24 << 20
VMEM_LIMIT = 24 << 20
GRAFT_LIMIT = 8 << 20
PICK_LIMIT = 8 << 20
HALF = 128
NEAR = (0, 4, 12, 2)
FAR = ((8, 9, 6, 7), (10, 11, 14, 15))
ORDER = NEAR + tuple(bits + 1 for bits in NEAR) + FAR[0] + FAR[1]
GROUPS = tuple(
    tuple(4 * x + offset for x in some) for offset in (0, 2, 1, 3) for some in ((0, 1, 3), (2,))
)


def dot(left, right, contract=ROWS_BY_COLUMNS):
    return lax.dot_general(left, right, contract, preferred_element_type=jnp.float32)


def split(matrix):
    high = matrix.astype(jnp.bfloat16)
    return high, (matrix - high.astype(jnp.float32)).astype(jnp.bfloat16)


def product(left, right, contract=ROWS_BY_COLUMNS):
    (left_high, left_low), (right_high, right_low) = left, right
    return dot(left_high, right_high, contract) + (
        dot(left_high, right_low, contract) + dot(left_low, right_high, contract)
    )


def cut_step(place_ref, grads_ref, mine_ref, *refs):
    near, sems = refs[:-1], refs[-1]
    shard, odd = place_ref[0, 1], place_ref[0, 2]
    mine = pl.ds(pl.multiple_of(odd * HALF, HALF), HALF)
    theirs = pl.ds(pl.multiple_of((1 - odd) * HALF, HALF), HALF)
    shards = mine_ref.shape[0]
    copies = []
    for step in range(shards):
        source = grads_ref.at[mine, pl.ds(step * BLK, BLK)]
        copies.append(pltpu.make_async_copy(source, mine_ref.at[step], sems.at[step]))
    for slot, out_ref in enumerate(near):
        for core in range(2):
            block = shard ^ (NEAR[slot] + core)
            source = grads_ref.at[theirs, pl.ds(pl.multiple_of(block * BLK, BLK), BLK)]
            sem = sems.at[shards + 2 * slot + core]
            copies.append(pltpu.make_async_copy(source, out_ref.at[core], sem))
    for copy in copies:
        copy.start()
    for copy in copies:
        copy.wait()


def cut(place, grads):
    shards = grads.shape[1] // BLK
    near = jax.ShapeDtypeStruct((2, HALF, BLK), grads.dtype)
    return pl.pallas_call(
        cut_step,
        out_shape=[jax.ShapeDtypeStruct((shards, HALF, BLK), grads.dtype)] + [near] * len(NEAR),
        in_specs=[pl.BlockSpec(memory_space=pltpu.SMEM), pl.BlockSpec(memory_space=pl.ANY)],
        out_specs=[pl.BlockSpec(memory_space=pltpu.VMEM)] * (1 + len(NEAR)),
        scratch_shapes=[pltpu.SemaphoreType.DMA((shards + 2 * len(NEAR),))],
        compiler_params=pltpu.CompilerParams(vmem_limit_bytes=CUT_LIMIT),
    )(place, grads)


def pick_step(place_ref, mine_ref, *outs):
    shard = place_ref[0, 1]
    for out_ref, some in zip(outs, FAR, strict=True):
        for slot, bits in enumerate(some):
            out_ref[slot] = mine_ref[shard ^ bits]


def pick(place, mine):
    vmem = pl.BlockSpec(memory_space=pltpu.VMEM)
    return pl.pallas_call(
        pick_step,
        out_shape=[jax.ShapeDtypeStruct((len(some),) + mine.shape[1:], mine.dtype) for some in FAR],
        in_specs=[pl.BlockSpec(memory_space=pltpu.SMEM), vmem],
        out_specs=[vmem] * len(FAR),
        compiler_params=pltpu.CompilerParams(vmem_limit_bytes=PICK_LIMIT),
    )(place, mine)


def half_step(place_ref, mine_ref, *refs):
    acts, (partial_ref, rest_ref, acts_ref) = refs[:-3], refs[-3:]
    shard, odd = place_ref[0, 1], place_ref[0, 2]
    mine = pl.ds(pl.multiple_of(odd * HALF, HALF), HALF)
    theirs = pl.ds(pl.multiple_of((1 - odd) * HALF, HALF), HALF)
    for group, group_ref in enumerate(acts):
        for slot, bits in enumerate(GROUPS[group]):
            columns = pl.ds(pl.multiple_of((shard ^ bits) * HALF, HALF), HALF)
            acts_ref[:, columns] = group_ref[slot, :, mine]
            rest_ref[:, pl.ds(ORDER.index(bits) * HALF, HALF)] = group_ref[slot, :, theirs]
    shards = mine_ref.shape[0]
    partial_ref[...] = dot(acts_ref[...], mine_ref[...].reshape(shards * HALF, BLK))


def half_gradient(place, mine, acts):
    vmem = pl.BlockSpec(memory_space=pltpu.VMEM)
    tokens = mine.shape[0] * HALF
    return pl.pallas_call(
        half_step,
        out_shape=(
            jax.ShapeDtypeStruct((BLK, BLK), jnp.float32),
            jax.ShapeDtypeStruct((BLK, tokens), mine.dtype),
        ),
        in_specs=[pl.BlockSpec(memory_space=pltpu.SMEM)] + [vmem] * (1 + len(acts)),
        out_specs=(vmem, vmem),
        scratch_shapes=[pltpu.VMEM((BLK, tokens), mine.dtype)],
        compiler_params=pltpu.CompilerParams(vmem_limit_bytes=HALF_LIMIT),
    )(place, mine, *acts)


def block_step(place_ref, partial_ref, rest_ref, *refs):
    near, others, (update_ref, sums_ref, root_ref) = refs[: len(NEAR)], refs[len(NEAR) : -3], refs[-3:]
    pieces = [jnp.concatenate([near_ref[0] for near_ref in near], axis=0)]
    pieces += [other_ref[...].reshape(-1, BLK) for other_ref in others]
    transposed = partial_ref[...]
    start = 0
    for piece in pieces:
        transposed = transposed + dot(rest_ref[:, start : start + piece.shape[0]], piece)
        start += piece.shape[0]
    parts = split(transposed)
    statistic = product(parts, parts, ROWS_BY_ROWS)
    grad_parts = split(transposed.T)
    on_diagonal = lax.broadcasted_iota(jnp.int32, (BLK, BLK), 0) == lax.broadcasted_iota(
        jnp.int32, (BLK, BLK), 1
    )
    shifted = statistic + jnp.where(on_diagonal, jnp.float32(SHIFT), jnp.float32(0.0))
    scaling = 2.5 / jnp.sqrt(jnp.sum(shifted * shifted) + 1e-06)
    root_ref[...] = jnp.where(on_diagonal, jnp.float32(1.25), jnp.float32(0.0)) - (
        0.25 * scaling
    ) * shifted

    @pl.when(place_ref[0, 0] == 2)
    def _():
        factor = root_ref[...]
        factor_parts = split(factor)
        square = product(factor_parts, factor_parts)
        square_parts = split(square)
        fourth = product(square_parts, square_parts)
        root_ref[...] = 1.25 * factor + product(split(fourth), split(square - 1.25 * factor))

    root_parts = split(root_ref[...])
    half = product(grad_parts, root_parts)
    update = product(split(half), root_parts) * jnp.sqrt(scaling)
    update_ref[...] = update
    lane = lax.broadcasted_iota(jnp.int32, sums_ref.shape, 2)
    grad_squares = jnp.sum(transposed * transposed)
    update_squares = jnp.sum(update * update)
    sums_ref[...] = jnp.where(lane == 0, grad_squares, jnp.where(lane == 1, update_squares, 0.0))


def run_block(place, partial, rest, pieces, devices):
    vmem = pl.BlockSpec(memory_space=pltpu.VMEM)
    return pl.pallas_call(
        block_step,
        out_shape=(
            jax.ShapeDtypeStruct((BLK, BLK), jnp.float32),
            jax.ShapeDtypeStruct((devices, 1, 128), jnp.float32),
        ),
        in_specs=[pl.BlockSpec(memory_space=pltpu.SMEM)] + [vmem] * (2 + len(pieces)),
        out_specs=(vmem, vmem),
        scratch_shapes=[pltpu.VMEM((BLK, BLK), jnp.float32)],
        compiler_params=pltpu.CompilerParams(vmem_limit_bytes=VMEM_LIMIT),
    )(place, partial, rest, *pieces)


def graft_step(sums_ref, update_ref, out_ref):
    totals = jnp.sum(sums_ref[...], axis=0)
    lane = lax.broadcasted_iota(jnp.int32, totals.shape, 1)
    grad_squares = jnp.sum(jnp.where(lane == 0, totals, 0.0))
    update_squares = jnp.sum(jnp.where(lane == 1, totals, 0.0))
    out_ref[...] = update_ref[...] * jnp.sqrt(grad_squares / update_squares)


def graft(sums, update):
    vmem = pl.BlockSpec(memory_space=pltpu.VMEM)
    return pl.pallas_call(
        graft_step,
        out_shape=jax.ShapeDtypeStruct(update.shape, update.dtype),
        in_specs=[vmem, vmem],
        out_specs=vmem,
        compiler_params=pltpu.CompilerParams(vmem_limit_bytes=GRAFT_LIMIT),
    )(sums, update)


def swap(value, axes, bits):
    size = 1
    for axis in axes:
        size *= lax.axis_size(axis)
    return lax.ppermute(value, axes, [(i, i ^ bits) for i in range(size)])


def swap_planes(value, up):
    step = 1 if up else -1
    pairs = [(i, (i + (step if i % 2 == 0 else -step)) % 8) for i in range(8)]
    return lax.ppermute(value, "prec", pairs)


def per_device(activations, output_grads, iter_counts):
    odd = lax.axis_index("prec") % 2
    place = jnp.stack([iter_counts[0, 0], lax.axis_index(DP), odd]).reshape(1, 3).astype(jnp.int32)
    own = activations.T
    near = [swap(own, ("x",), bits) for bits in (1, 3)]
    mine, here, *near_grads = cut(place, output_grads)
    three = jnp.stack([own] + near)
    mine, three = lax.optimization_barrier((mine, three))
    mine = lax.all_to_all(mine, DP, 0, 0, tiled=True)
    three_y = swap(three, ("yl", "pair"), 3)
    last = swap(three[1:2], ("x",), 3)
    far_three = [swap(value, ("core",), 1) for value in (three, three_y)]
    ready, _ = lax.optimization_barrier((mine, far_three))
    first, second = pick(place, ready)
    last, _ = lax.optimization_barrier((last, (first, second)))
    ways = (("x", 1), ("x", 3), ("yl", 1))
    near_grads, _ = lax.optimization_barrier((near_grads, (first, second)))
    near_grads = [swap(value, (axis,), bits) for value, (axis, bits) in zip(near_grads, ways, strict=True)]
    first, second = swap_planes(first, True), swap_planes(second, False)
    last_y = swap(last, ("yl", "pair"), 3)
    far_last = [swap(value, ("core",), 1) for value in (last, last_y)]
    acts = [three, last, three_y, last_y, far_three[0], far_last[0], far_three[1], far_last[1]]
    near_grads, _ = lax.optimization_barrier((near_grads, (first, second)))
    near_grads = [here] + near_grads
    taken = swap(jnp.stack([value[1] for value in near_grads]), ("core",), 1)
    partial, rest = half_gradient(place, mine, acts)

    devices = 256
    update, sums = run_block(place, partial, rest, (*near_grads, taken, first, second), devices)
    sums = lax.all_to_all(sums, EVERY, 0, 0, tiled=True)
    return graft(sums, update)


def solution(mesh):
    fine = Mesh(mesh.devices.reshape(4, 2, 2, 8, 2), EVERY)
    in_specs = (P(DP, "prec"), P(DP, "pair"), P(("pair",) + DP, "prec"))
    out_specs = P(("pair",) + DP, "prec")
    return jax.shard_map(
        per_device, mesh=fine, in_specs=in_specs, out_specs=out_specs, check_vma=False
    )
```

```python
import jax
import jax.numpy as jnp
from jax import lax
from jax.experimental import pallas as pl
from jax.experimental.pallas import tpu as pltpu
from jax.sharding import Mesh, PartitionSpec as P

BLK = 512
SHIFT = 0.001
DP = ("x", "yl", "core")
EVERY = ("x", "yl", "core", "prec", "pair")
ROWS_BY_ROWS = (((1,), (1,)), ((), ()))
ROWS_BY_COLUMNS = (((1,), (0,)), ((), ()))
CUT_LIMIT = 48 << 20
HALF_LIMIT = 24 << 20
VMEM_LIMIT = 24 << 20
GRAFT_LIMIT = 8 << 20
PICK_LIMIT = 8 << 20
HALF = 128
NEAR = (0, 4, 12, 2)
FAR = ((8, 9, 6, 7), (10, 11, 14, 15))
LATE = (8, 10, 9, 11)
ORDER = NEAR + tuple(bits + 1 for bits in NEAR) + FAR[0][2:] + FAR[1][2:]
GROUPS = tuple(tuple(4 * x + offset for x in (0, 1, 3)) for offset in (0, 2, 1, 3))


def dot(left, right, contract=ROWS_BY_COLUMNS):
    return lax.dot_general(left, right, contract, preferred_element_type=jnp.float32)


def split(matrix):
    high = matrix.astype(jnp.bfloat16)
    return high, (matrix - high.astype(jnp.float32)).astype(jnp.bfloat16)


def product(left, right, contract=ROWS_BY_COLUMNS):
    (left_high, left_low), (right_high, right_low) = left, right
    return dot(left_high, right_high, contract) + (
        dot(left_high, right_low, contract) + dot(left_low, right_high, contract)
    )


def cut_step(place_ref, grads_ref, mine_ref, *refs):
    near, sems = refs[:-1], refs[-1]
    shard, odd = place_ref[0, 1], place_ref[0, 2]
    mine = pl.ds(pl.multiple_of(odd * HALF, HALF), HALF)
    theirs = pl.ds(pl.multiple_of((1 - odd) * HALF, HALF), HALF)
    shards = mine_ref.shape[0]
    copies = []
    for step in range(shards):
        source = grads_ref.at[mine, pl.ds(step * BLK, BLK)]
        copies.append(pltpu.make_async_copy(source, mine_ref.at[step], sems.at[step]))
    for slot, out_ref in enumerate(near):
        for core in range(2):
            block = shard ^ (NEAR[slot] + core)
            source = grads_ref.at[theirs, pl.ds(pl.multiple_of(block * BLK, BLK), BLK)]
            sem = sems.at[shards + 2 * slot + core]
            copies.append(pltpu.make_async_copy(source, out_ref.at[core], sem))
    for copy in copies:
        copy.start()
    for copy in copies:
        copy.wait()


def cut(place, grads):
    shards = grads.shape[1] // BLK
    near = jax.ShapeDtypeStruct((2, HALF, BLK), grads.dtype)
    return pl.pallas_call(
        cut_step,
        out_shape=[jax.ShapeDtypeStruct((shards, HALF, BLK), grads.dtype)] + [near] * len(NEAR),
        in_specs=[pl.BlockSpec(memory_space=pltpu.SMEM), pl.BlockSpec(memory_space=pl.ANY)],
        out_specs=[pl.BlockSpec(memory_space=pltpu.VMEM)] * (1 + len(NEAR)),
        scratch_shapes=[pltpu.SemaphoreType.DMA((shards + 2 * len(NEAR),))],
        compiler_params=pltpu.CompilerParams(vmem_limit_bytes=CUT_LIMIT),
    )(place, grads)


def pick_step(place_ref, mine_ref, *outs):
    shard = place_ref[0, 1]
    for out_ref, some in zip(outs, FAR, strict=True):
        for slot, bits in enumerate(some):
            out_ref[slot] = mine_ref[shard ^ bits]


def pick(place, mine):
    vmem = pl.BlockSpec(memory_space=pltpu.VMEM)
    return pl.pallas_call(
        pick_step,
        out_shape=[jax.ShapeDtypeStruct((len(some),) + mine.shape[1:], mine.dtype) for some in FAR],
        in_specs=[pl.BlockSpec(memory_space=pltpu.SMEM), vmem],
        out_specs=[vmem] * len(FAR),
        compiler_params=pltpu.CompilerParams(vmem_limit_bytes=PICK_LIMIT),
    )(place, mine)


def half_step(place_ref, mine_ref, *refs):
    acts, (partial_ref, rest_ref, acts_ref) = refs[:-3], refs[-3:]
    shard, odd = place_ref[0, 1], place_ref[0, 2]
    mine = pl.ds(pl.multiple_of(odd * HALF, HALF), HALF)
    theirs = pl.ds(pl.multiple_of((1 - odd) * HALF, HALF), HALF)
    for group, group_ref in enumerate(acts):
        for slot, bits in enumerate(GROUPS[group]):
            columns = pl.ds(ORDER.index(bits) * HALF, HALF)
            acts_ref[:, columns] = group_ref[slot, :, mine]
            rest_ref[:, columns] = group_ref[slot, :, theirs]
    blocks = jnp.concatenate([mine_ref[shard ^ bits] for bits in ORDER], axis=0)
    partial_ref[...] = dot(acts_ref[...], blocks)


def half_gradient(place, mine, acts):
    vmem = pl.BlockSpec(memory_space=pltpu.VMEM)
    tokens = len(ORDER) * HALF
    return pl.pallas_call(
        half_step,
        out_shape=(
            jax.ShapeDtypeStruct((BLK, BLK), jnp.float32),
            jax.ShapeDtypeStruct((BLK, tokens), mine.dtype),
        ),
        in_specs=[pl.BlockSpec(memory_space=pltpu.SMEM)] + [vmem] * (1 + len(acts)),
        out_specs=(vmem, vmem),
        scratch_shapes=[pltpu.VMEM((BLK, tokens), mine.dtype)],
        compiler_params=pltpu.CompilerParams(vmem_limit_bytes=HALF_LIMIT),
    )(place, mine, *acts)


def block_step(place_ref, partial_ref, rest_ref, *refs):
    late, mine, (first_ref, second_ref, taken_ref) = refs[:4], refs[4:6], refs[6:9]
    near, (update_ref, sums_ref, root_ref) = refs[9:-3], refs[-3:]
    odd = place_ref[0, 2] == 1
    transposed = partial_ref[...]
    for act_ref, bits in zip(late, LATE, strict=True):
        part = bits // 2 % 2
        own = mine[part][bits % 2]
        other = (first_ref, second_ref)[part][bits % 2]
        piece = [jnp.where(odd, other, own), jnp.where(odd, own, other)]
        transposed = transposed + dot(act_ref[0], jnp.concatenate(piece, axis=0))
    pieces = [jnp.concatenate([near_ref[0] for near_ref in near], axis=0)]
    pieces += [taken_ref[...].reshape(-1, BLK)]
    pieces += [jnp.concatenate([ref[2], ref[3]], axis=0) for ref in (first_ref, second_ref)]
    start = 0
    for piece in pieces:
        transposed = transposed + dot(rest_ref[:, start : start + piece.shape[0]], piece)
        start += piece.shape[0]
    parts = split(transposed)
    statistic = product(parts, parts, ROWS_BY_ROWS)
    grad_parts = split(transposed.T)
    on_diagonal = lax.broadcasted_iota(jnp.int32, (BLK, BLK), 0) == lax.broadcasted_iota(
        jnp.int32, (BLK, BLK), 1
    )
    shifted = statistic + jnp.where(on_diagonal, jnp.float32(SHIFT), jnp.float32(0.0))
    scaling = 2.5 / jnp.sqrt(jnp.sum(shifted * shifted) + 1e-06)
    root_ref[...] = jnp.where(on_diagonal, jnp.float32(1.25), jnp.float32(0.0)) - (
        0.25 * scaling
    ) * shifted

    @pl.when(place_ref[0, 0] == 2)
    def _():
        factor = root_ref[...]
        factor_parts = split(factor)
        square = product(factor_parts, factor_parts)
        square_parts = split(square)
        fourth = product(square_parts, square_parts)
        root_ref[...] = 1.25 * factor + product(split(fourth), split(square - 1.25 * factor))

    root_parts = split(root_ref[...])
    half = product(grad_parts, root_parts)
    update = product(split(half), root_parts) * jnp.sqrt(scaling)
    update_ref[...] = update
    lane = lax.broadcasted_iota(jnp.int32, sums_ref.shape, 2)
    grad_squares = jnp.sum(transposed * transposed)
    update_squares = jnp.sum(update * update)
    sums_ref[...] = jnp.where(lane == 0, grad_squares, jnp.where(lane == 1, update_squares, 0.0))


def run_block(place, partial, rest, pieces, devices):
    vmem = pl.BlockSpec(memory_space=pltpu.VMEM)
    return pl.pallas_call(
        block_step,
        out_shape=(
            jax.ShapeDtypeStruct((BLK, BLK), jnp.float32),
            jax.ShapeDtypeStruct((devices, 1, 128), jnp.float32),
        ),
        in_specs=[pl.BlockSpec(memory_space=pltpu.SMEM)] + [vmem] * (2 + len(pieces)),
        out_specs=(vmem, vmem),
        scratch_shapes=[pltpu.VMEM((BLK, BLK), jnp.float32)],
        compiler_params=pltpu.CompilerParams(vmem_limit_bytes=VMEM_LIMIT),
    )(place, partial, rest, *pieces)


def graft_step(sums_ref, update_ref, out_ref):
    totals = jnp.sum(sums_ref[...], axis=0)
    lane = lax.broadcasted_iota(jnp.int32, totals.shape, 1)
    grad_squares = jnp.sum(jnp.where(lane == 0, totals, 0.0))
    update_squares = jnp.sum(jnp.where(lane == 1, totals, 0.0))
    out_ref[...] = update_ref[...] * jnp.sqrt(grad_squares / update_squares)


def graft(sums, update):
    vmem = pl.BlockSpec(memory_space=pltpu.VMEM)
    return pl.pallas_call(
        graft_step,
        out_shape=jax.ShapeDtypeStruct(update.shape, update.dtype),
        in_specs=[vmem, vmem],
        out_specs=vmem,
        compiler_params=pltpu.CompilerParams(vmem_limit_bytes=GRAFT_LIMIT),
    )(sums, update)


def swap(value, axes, bits):
    size = 1
    for axis in axes:
        size *= lax.axis_size(axis)
    return lax.ppermute(value, axes, [(i, i ^ bits) for i in range(size)])


def swap_planes(value, up):
    step = 1 if up else -1
    pairs = [(i, (i + (step if i % 2 == 0 else -step)) % 8) for i in range(8)]
    return lax.ppermute(value, "prec", pairs)


def per_device(activations, output_grads, iter_counts):
    odd = lax.axis_index("prec") % 2
    place = jnp.stack([iter_counts[0, 0], lax.axis_index(DP), odd]).reshape(1, 3).astype(jnp.int32)
    own = activations.T
    near = [swap(own, ("x",), bits) for bits in (1, 3)]
    mine, here, *near_grads = cut(place, output_grads)
    three = jnp.stack([own] + near)
    mine, three = lax.optimization_barrier((mine, three))
    mine = lax.all_to_all(mine, DP, 0, 0, tiled=True)
    three_y = swap(three, ("yl", "pair"), 3)
    last = swap(three[1:2], ("x",), 3)
    far_three = [swap(value, ("core",), 1) for value in (three, three_y)]
    ready, _ = lax.optimization_barrier((mine, far_three))
    first, second = pick(place, ready)
    last, _ = lax.optimization_barrier((last, (first, second)))
    ways = (("x", 1), ("x", 3), ("yl", 1))
    near_grads, _ = lax.optimization_barrier((near_grads, (first, second)))
    near_grads = [swap(value, (axis,), bits) for value, (axis, bits) in zip(near_grads, ways, strict=True)]
    picked = first, second
    first, second = swap_planes(first, True), swap_planes(second, False)
    last_y = swap(last, ("yl", "pair"), 3)
    far_last = [swap(value, ("core",), 1) for value in (last, last_y)]
    acts = [three, three_y, *far_three]
    late = [last, last_y, *far_last]
    near_grads, _ = lax.optimization_barrier((near_grads, (first, second)))
    near_grads = [here] + near_grads
    taken = swap(jnp.stack([value[1] for value in near_grads]), ("core",), 1)
    partial, rest = half_gradient(place, mine, acts)

    devices = 256
    update, sums = run_block(place, partial, rest, (*late, *picked, first, second, taken, *near_grads), devices)
    sums = lax.all_to_all(sums, EVERY, 0, 0, tiled=True)
    return graft(sums, update)


def solution(mesh):
    fine = Mesh(mesh.devices.reshape(4, 2, 2, 8, 2), EVERY)
    in_specs = (P(DP, "prec"), P(DP, "pair"), P(("pair",) + DP, "prec"))
    out_specs = P(("pair",) + DP, "prec")
    return jax.shard_map(
        per_device, mesh=fine, in_specs=in_specs, out_specs=out_specs, check_vma=False
    )
```

```python
import jax
import jax.numpy as jnp
from jax import lax
from jax.experimental import pallas as pl
from jax.experimental.pallas import tpu as pltpu
from jax.sharding import Mesh, PartitionSpec as P

BLK = 512
SHIFT = 0.001
DP = ("x", "yl", "core")
EVERY = ("x", "yl", "core", "prec", "pair")
ROWS_BY_ROWS = (((1,), (1,)), ((), ()))
ROWS_BY_COLUMNS = (((1,), (0,)), ((), ()))
CUT_LIMIT = 48 << 20
HALF_LIMIT = 24 << 20
VMEM_LIMIT = 24 << 20
GRAFT_LIMIT = 8 << 20
PICK_LIMIT = 8 << 20
HALF = 128
NEAR = (0, 4, 12, 2)
FAR = ((8, 9, 6, 7), (10, 11, 14, 15))
LATE = (8, 10, 9, 11)
ORDER = NEAR + tuple(bits + 1 for bits in NEAR) + FAR[0][2:] + FAR[1][2:]
GROUPS = tuple(tuple(4 * x + offset for x in (0, 1, 3)) for offset in (0, 2, 1, 3))


def dot(left, right, contract=ROWS_BY_COLUMNS):
    return lax.dot_general(left, right, contract, preferred_element_type=jnp.float32)


def split(matrix):
    high = matrix.astype(jnp.bfloat16)
    return high, (matrix - high.astype(jnp.float32)).astype(jnp.bfloat16)


def product(left, right, contract=ROWS_BY_COLUMNS):
    (left_high, left_low), (right_high, right_low) = left, right
    return dot(left_high, right_high, contract) + (
        dot(left_high, right_low, contract) + dot(left_low, right_high, contract)
    )


def cut_step(place_ref, grads_ref, mine_ref, *refs):
    near, sems = refs[:-1], refs[-1]
    shard, odd = place_ref[0, 1], place_ref[0, 2]
    mine = pl.ds(pl.multiple_of(odd * HALF, HALF), HALF)
    theirs = pl.ds(pl.multiple_of((1 - odd) * HALF, HALF), HALF)
    shards = mine_ref.shape[0]
    copies = []
    for step in range(shards):
        source = grads_ref.at[mine, pl.ds(step * BLK, BLK)]
        copies.append(pltpu.make_async_copy(source, mine_ref.at[step], sems.at[step]))
    for slot, out_ref in enumerate(near):
        for core in range(2):
            block = shard ^ (NEAR[slot] + core)
            source = grads_ref.at[theirs, pl.ds(pl.multiple_of(block * BLK, BLK), BLK)]
            sem = sems.at[shards + 2 * slot + core]
            copies.append(pltpu.make_async_copy(source, out_ref.at[core], sem))
    for copy in copies:
        copy.start()
    for copy in copies:
        copy.wait()


def cut(place, grads):
    shards = grads.shape[1] // BLK
    near = jax.ShapeDtypeStruct((2, HALF, BLK), grads.dtype)
    return pl.pallas_call(
        cut_step,
        out_shape=[jax.ShapeDtypeStruct((shards, HALF, BLK), grads.dtype)] + [near] * len(NEAR),
        in_specs=[pl.BlockSpec(memory_space=pltpu.SMEM), pl.BlockSpec(memory_space=pl.ANY)],
        out_specs=[pl.BlockSpec(memory_space=pltpu.VMEM)] * (1 + len(NEAR)),
        scratch_shapes=[pltpu.SemaphoreType.DMA((shards + 2 * len(NEAR),))],
        compiler_params=pltpu.CompilerParams(vmem_limit_bytes=CUT_LIMIT),
    )(place, grads)


def pick_step(place_ref, mine_ref, *outs):
    shard = place_ref[0, 1]
    for out_ref, some in zip(outs, FAR, strict=True):
        for slot, bits in enumerate(some):
            out_ref[slot] = mine_ref[shard ^ bits]


def pick(place, mine):
    vmem = pl.BlockSpec(memory_space=pltpu.VMEM)
    return pl.pallas_call(
        pick_step,
        out_shape=[jax.ShapeDtypeStruct((len(some),) + mine.shape[1:], mine.dtype) for some in FAR],
        in_specs=[pl.BlockSpec(memory_space=pltpu.SMEM), vmem],
        out_specs=[vmem] * len(FAR),
        compiler_params=pltpu.CompilerParams(vmem_limit_bytes=PICK_LIMIT),
    )(place, mine)


def half_step(place_ref, mine_ref, *refs):
    acts, (partial_ref, rest_ref, acts_ref) = refs[:-3], refs[-3:]
    shard, odd = place_ref[0, 1], place_ref[0, 2]
    mine = pl.ds(pl.multiple_of(odd * HALF, HALF), HALF)
    theirs = pl.ds(pl.multiple_of((1 - odd) * HALF, HALF), HALF)
    for group, group_ref in enumerate(acts):
        for slot, bits in enumerate(GROUPS[group]):
            columns = pl.ds(ORDER.index(bits) * HALF, HALF)
            acts_ref[:, columns] = group_ref[slot, :, mine]
            rest_ref[:, columns] = group_ref[slot, :, theirs]
    blocks = jnp.concatenate([mine_ref[shard ^ bits] for bits in ORDER], axis=0)
    partial_ref[...] = dot(acts_ref[...], blocks)


def half_gradient(place, mine, acts):
    vmem = pl.BlockSpec(memory_space=pltpu.VMEM)
    tokens = len(ORDER) * HALF
    return pl.pallas_call(
        half_step,
        out_shape=(
            jax.ShapeDtypeStruct((BLK, BLK), jnp.float32),
            jax.ShapeDtypeStruct((BLK, tokens), mine.dtype),
        ),
        in_specs=[pl.BlockSpec(memory_space=pltpu.SMEM)] + [vmem] * (1 + len(acts)),
        out_specs=(vmem, vmem),
        scratch_shapes=[pltpu.VMEM((BLK, tokens), mine.dtype)],
        compiler_params=pltpu.CompilerParams(vmem_limit_bytes=HALF_LIMIT),
    )(place, mine, *acts)


def block_step(place_ref, partial_ref, rest_ref, *refs):
    late, mine, (first_ref, second_ref, taken_ref) = refs[:4], refs[4:6], refs[6:9]
    near, (update_ref, sums_ref, root_ref) = refs[9:-3], refs[-3:]
    odd = place_ref[0, 2] == 1
    transposed = partial_ref[...]
    for act_ref, bits in zip(late, LATE, strict=True):
        part = bits // 2 % 2
        own = mine[part][bits % 2]
        other = (first_ref, second_ref)[part][bits % 2]
        piece = [jnp.where(odd, other, own), jnp.where(odd, own, other)]
        transposed = transposed + dot(act_ref[0], jnp.concatenate(piece, axis=0))
    pieces = [jnp.concatenate([near_ref[0] for near_ref in near], axis=0)]
    pieces += [taken_ref[...].reshape(-1, BLK)]
    pieces += [jnp.concatenate([ref[2], ref[3]], axis=0) for ref in (first_ref, second_ref)]
    start = 0
    for piece in pieces:
        transposed = transposed + dot(rest_ref[:, start : start + piece.shape[0]], piece)
        start += piece.shape[0]
    parts = split(transposed)
    statistic = product(parts, parts, ROWS_BY_ROWS)
    grad_parts = split(transposed.T)
    on_diagonal = lax.broadcasted_iota(jnp.int32, (BLK, BLK), 0) == lax.broadcasted_iota(
        jnp.int32, (BLK, BLK), 1
    )
    shifted = statistic + jnp.where(on_diagonal, jnp.float32(SHIFT), jnp.float32(0.0))
    scaling = 2.5 / jnp.sqrt(jnp.sum(shifted * shifted) + 1e-06)
    root_ref[...] = jnp.where(on_diagonal, jnp.float32(1.25), jnp.float32(0.0)) - (
        0.25 * scaling
    ) * shifted

    @pl.when(place_ref[0, 0] == 2)
    def _():
        factor = root_ref[...]
        factor_parts = split(factor)
        square = product(factor_parts, factor_parts)
        square_parts = split(square)
        fourth = product(square_parts, square_parts)
        root_ref[...] = 1.25 * factor + product(split(fourth), split(square - 1.25 * factor))

    root_parts = split(root_ref[...])
    half = product(grad_parts, root_parts)
    update = product(split(half), root_parts) * jnp.sqrt(scaling)
    update_ref[...] = update
    lane = lax.broadcasted_iota(jnp.int32, sums_ref.shape, 2)
    grad_squares = jnp.sum(transposed * transposed)
    update_squares = jnp.sum(update * update)
    sums_ref[...] = jnp.where(lane == 0, grad_squares, jnp.where(lane == 1, update_squares, 0.0))


def run_block(place, partial, rest, pieces, devices):
    vmem = pl.BlockSpec(memory_space=pltpu.VMEM)
    return pl.pallas_call(
        block_step,
        out_shape=(
            jax.ShapeDtypeStruct((BLK, BLK), jnp.float32),
            jax.ShapeDtypeStruct((devices, 1, 128), jnp.float32),
        ),
        in_specs=[pl.BlockSpec(memory_space=pltpu.SMEM)] + [vmem] * (2 + len(pieces)),
        out_specs=(vmem, vmem),
        scratch_shapes=[pltpu.VMEM((BLK, BLK), jnp.float32)],
        compiler_params=pltpu.CompilerParams(vmem_limit_bytes=VMEM_LIMIT),
    )(place, partial, rest, *pieces)


def graft_step(sums_ref, update_ref, out_ref):
    totals = jnp.sum(sums_ref[...], axis=0)
    lane = lax.broadcasted_iota(jnp.int32, totals.shape, 1)
    grad_squares = jnp.sum(jnp.where(lane == 0, totals, 0.0))
    update_squares = jnp.sum(jnp.where(lane == 1, totals, 0.0))
    out_ref[...] = update_ref[...] * jnp.sqrt(grad_squares / update_squares)


def graft(sums, update):
    vmem = pl.BlockSpec(memory_space=pltpu.VMEM)
    return pl.pallas_call(
        graft_step,
        out_shape=jax.ShapeDtypeStruct(update.shape, update.dtype),
        in_specs=[vmem, vmem],
        out_specs=vmem,
        compiler_params=pltpu.CompilerParams(vmem_limit_bytes=GRAFT_LIMIT),
    )(sums, update)


def swap(value, axes, bits):
    size = 1
    for axis in axes:
        size *= lax.axis_size(axis)
    return lax.ppermute(value, axes, [(i, i ^ bits) for i in range(size)])


def swap_planes(value, up):
    step = 1 if up else -1
    pairs = [(i, (i + (step if i % 2 == 0 else -step)) % 8) for i in range(8)]
    return lax.ppermute(value, "prec", pairs)


def per_device(activations, output_grads, iter_counts):
    odd = lax.axis_index("prec") % 2
    place = jnp.stack([iter_counts[0, 0], lax.axis_index(DP), odd]).reshape(1, 3).astype(jnp.int32)
    own = activations.T
    near = [swap(own, ("x",), bits) for bits in (1, 3)]
    mine, here, *near_grads = cut(place, output_grads)
    three = jnp.stack([own] + near)
    mine, three = lax.optimization_barrier((mine, three))
    mine = lax.all_to_all(mine, DP, 0, 0, tiled=True)
    three_y = swap(three, ("yl", "pair"), 3)
    last = swap(three[1:2], ("x",), 3)
    far_three = [swap(value, ("core",), 1) for value in (three, three_y)]
    ready, _ = lax.optimization_barrier((mine, far_three))
    first, second = pick(place, ready)
    last, _ = lax.optimization_barrier((last, (first, second)))
    ways = (("x", 1), ("x", 3), ("yl", 1))
    near_grads, _ = lax.optimization_barrier((near_grads, (first, second)))
    near_grads = [swap(value, (axis,), bits) for value, (axis, bits) in zip(near_grads, ways, strict=True)]
    picked = first, second
    first, second = swap_planes(first, True), swap_planes(second, False)
    last_y = swap(last, ("yl", "pair"), 3)
    far_last = [swap(value, ("core",), 1) for value in (last, last_y)]
    acts = [three, three_y, *far_three]
    late = [last, last_y, *far_last]
    near_grads, _ = lax.optimization_barrier((near_grads, (first, second)))
    near_grads = [here] + near_grads
    partial, rest = half_gradient(place, mine, acts)
    leaving, _ = lax.optimization_barrier((jnp.stack([value[1] for value in near_grads]), partial))
    taken = swap(leaving, ("core",), 1)

    devices = 256
    update, sums = run_block(place, partial, rest, (*late, *picked, first, second, taken, *near_grads), devices)
    sums = lax.all_to_all(sums, EVERY, 0, 0, tiled=True)
    return graft(sums, update)


def solution(mesh):
    fine = Mesh(mesh.devices.reshape(4, 2, 2, 8, 2), EVERY)
    in_specs = (P(DP, "prec"), P(DP, "pair"), P(("pair",) + DP, "prec"))
    out_specs = P(("pair",) + DP, "prec")
    return jax.shard_map(
        per_device, mesh=fine, in_specs=in_specs, out_specs=out_specs, check_vma=False
    )
```

```python
import jax
import jax.numpy as jnp
from jax import lax
from jax.experimental import pallas as pl
from jax.experimental.pallas import tpu as pltpu
from jax.sharding import Mesh, PartitionSpec as P

BLK = 512
SHIFT = 0.001
DP = ("x", "yl", "core")
EVERY = ("x", "yl", "core", "prec", "pair")
ROWS_BY_ROWS = (((1,), (1,)), ((), ()))
ROWS_BY_COLUMNS = (((1,), (0,)), ((), ()))
CUT_LIMIT = 48 << 20
HALF_LIMIT = 24 << 20
VMEM_LIMIT = 24 << 20
GRAFT_LIMIT = 8 << 20
PICK_LIMIT = 8 << 20
HALF = 128
NEAR = (0, 4, 12, 2)
FAR = ((8, 9, 6, 7), (10, 11, 14, 15))
LATE = (8, 10, 9, 11)
ORDER = NEAR + tuple(bits + 1 for bits in NEAR) + FAR[0][2:] + FAR[1][2:]
GROUPS = tuple(tuple(4 * x + offset for x in (0, 1, 3)) for offset in (0, 2, 1, 3))


def dot(left, right, contract=ROWS_BY_COLUMNS):
    return lax.dot_general(left, right, contract, preferred_element_type=jnp.float32)


def split(matrix):
    high = matrix.astype(jnp.bfloat16)
    return high, (matrix - high.astype(jnp.float32)).astype(jnp.bfloat16)


def product(left, right, contract=ROWS_BY_COLUMNS):
    (left_high, left_low), (right_high, right_low) = left, right
    axis = contract[0][1][0]
    return dot(
        jnp.concatenate([left_high, left_low, left_high], axis=1),
        jnp.concatenate([right_high, right_high, right_low], axis=axis),
        contract,
    )


def cut_step(place_ref, grads_ref, mine_ref, *refs):
    near, sems = refs[:-1], refs[-1]
    shard, odd = place_ref[0, 1], place_ref[0, 2]
    mine = pl.ds(pl.multiple_of(odd * HALF, HALF), HALF)
    theirs = pl.ds(pl.multiple_of((1 - odd) * HALF, HALF), HALF)
    shards = mine_ref.shape[0]
    copies = []
    for step in range(shards):
        source = grads_ref.at[mine, pl.ds(step * BLK, BLK)]
        copies.append(pltpu.make_async_copy(source, mine_ref.at[step], sems.at[step]))
    for slot, out_ref in enumerate(near):
        for core in range(2):
            block = shard ^ (NEAR[slot] + core)
            source = grads_ref.at[theirs, pl.ds(pl.multiple_of(block * BLK, BLK), BLK)]
            sem = sems.at[shards + 2 * slot + core]
            copies.append(pltpu.make_async_copy(source, out_ref.at[core], sem))
    for copy in copies:
        copy.start()
    for copy in copies:
        copy.wait()


def cut(place, grads):
    shards = grads.shape[1] // BLK
    near = jax.ShapeDtypeStruct((2, HALF, BLK), grads.dtype)
    return pl.pallas_call(
        cut_step,
        out_shape=[jax.ShapeDtypeStruct((shards, HALF, BLK), grads.dtype)] + [near] * len(NEAR),
        in_specs=[pl.BlockSpec(memory_space=pltpu.SMEM), pl.BlockSpec(memory_space=pl.ANY)],
        out_specs=[pl.BlockSpec(memory_space=pltpu.VMEM)] * (1 + len(NEAR)),
        scratch_shapes=[pltpu.SemaphoreType.DMA((shards + 2 * len(NEAR),))],
        compiler_params=pltpu.CompilerParams(vmem_limit_bytes=CUT_LIMIT),
    )(place, grads)


def pick_step(place_ref, mine_ref, *outs):
    shard = place_ref[0, 1]
    for out_ref, some in zip(outs, FAR, strict=True):
        for slot, bits in enumerate(some):
            out_ref[slot] = mine_ref[shard ^ bits]


def pick(place, mine):
    vmem = pl.BlockSpec(memory_space=pltpu.VMEM)
    return pl.pallas_call(
        pick_step,
        out_shape=[jax.ShapeDtypeStruct((len(some),) + mine.shape[1:], mine.dtype) for some in FAR],
        in_specs=[pl.BlockSpec(memory_space=pltpu.SMEM), vmem],
        out_specs=[vmem] * len(FAR),
        compiler_params=pltpu.CompilerParams(vmem_limit_bytes=PICK_LIMIT),
    )(place, mine)


def half_step(place_ref, mine_ref, *refs):
    acts, (partial_ref, rest_ref, acts_ref) = refs[:-3], refs[-3:]
    shard, odd = place_ref[0, 1], place_ref[0, 2]
    mine = pl.ds(pl.multiple_of(odd * HALF, HALF), HALF)
    theirs = pl.ds(pl.multiple_of((1 - odd) * HALF, HALF), HALF)
    for group, group_ref in enumerate(acts):
        for slot, bits in enumerate(GROUPS[group]):
            columns = pl.ds(ORDER.index(bits) * HALF, HALF)
            acts_ref[:, columns] = group_ref[slot, :, mine]
            rest_ref[:, columns] = group_ref[slot, :, theirs]
    blocks = jnp.concatenate([mine_ref[shard ^ bits] for bits in ORDER], axis=0)
    partial_ref[...] = dot(acts_ref[...], blocks)


def half_gradient(place, mine, acts):
    vmem = pl.BlockSpec(memory_space=pltpu.VMEM)
    tokens = len(ORDER) * HALF
    return pl.pallas_call(
        half_step,
        out_shape=(
            jax.ShapeDtypeStruct((BLK, BLK), jnp.float32),
            jax.ShapeDtypeStruct((BLK, tokens), mine.dtype),
        ),
        in_specs=[pl.BlockSpec(memory_space=pltpu.SMEM)] + [vmem] * (1 + len(acts)),
        out_specs=(vmem, vmem),
        scratch_shapes=[pltpu.VMEM((BLK, tokens), mine.dtype)],
        compiler_params=pltpu.CompilerParams(vmem_limit_bytes=HALF_LIMIT),
    )(place, mine, *acts)


def block_step(place_ref, partial_ref, rest_ref, *refs):
    late, mine, (first_ref, second_ref, taken_ref) = refs[:4], refs[4:6], refs[6:9]
    near, (update_ref, sums_ref, root_ref) = refs[9:-3], refs[-3:]
    odd = place_ref[0, 2] == 1
    transposed = partial_ref[...]
    for act_ref, bits in zip(late, LATE, strict=True):
        part = bits // 2 % 2
        own = mine[part][bits % 2]
        other = (first_ref, second_ref)[part][bits % 2]
        piece = [jnp.where(odd, other, own), jnp.where(odd, own, other)]
        transposed = transposed + dot(act_ref[0], jnp.concatenate(piece, axis=0))
    pieces = [jnp.concatenate([near_ref[0] for near_ref in near], axis=0)]
    pieces += [taken_ref[...].reshape(-1, BLK)]
    pieces += [jnp.concatenate([ref[2], ref[3]], axis=0) for ref in (first_ref, second_ref)]
    start = 0
    for piece in pieces:
        transposed = transposed + dot(rest_ref[:, start : start + piece.shape[0]], piece)
        start += piece.shape[0]
    parts = split(transposed)
    statistic = product(parts, parts, ROWS_BY_ROWS)
    grad_parts = split(transposed.T)
    on_diagonal = lax.broadcasted_iota(jnp.int32, (BLK, BLK), 0) == lax.broadcasted_iota(
        jnp.int32, (BLK, BLK), 1
    )
    shifted = statistic + jnp.where(on_diagonal, jnp.float32(SHIFT), jnp.float32(0.0))
    scaling = 2.5 / jnp.sqrt(jnp.sum(shifted * shifted) + 1e-06)
    root_ref[...] = jnp.where(on_diagonal, jnp.float32(1.25), jnp.float32(0.0)) - (
        0.25 * scaling
    ) * shifted

    @pl.when(place_ref[0, 0] == 2)
    def _():
        factor = root_ref[...]
        factor_parts = split(factor)
        square = product(factor_parts, factor_parts)
        square_parts = split(square)
        fourth = product(square_parts, square_parts)
        root_ref[...] = 1.25 * factor + product(split(fourth), split(square - 1.25 * factor))

    root_parts = split(root_ref[...])
    half = product(grad_parts, root_parts)
    update = product(split(half), root_parts) * jnp.sqrt(scaling)
    update_ref[...] = update
    lane = lax.broadcasted_iota(jnp.int32, sums_ref.shape, 2)
    grad_squares = jnp.sum(transposed * transposed)
    update_squares = jnp.sum(update * update)
    sums_ref[...] = jnp.where(lane == 0, grad_squares, jnp.where(lane == 1, update_squares, 0.0))


def run_block(place, partial, rest, pieces, devices):
    vmem = pl.BlockSpec(memory_space=pltpu.VMEM)
    return pl.pallas_call(
        block_step,
        out_shape=(
            jax.ShapeDtypeStruct((BLK, BLK), jnp.float32),
            jax.ShapeDtypeStruct((devices, 1, 128), jnp.float32),
        ),
        in_specs=[pl.BlockSpec(memory_space=pltpu.SMEM)] + [vmem] * (2 + len(pieces)),
        out_specs=(vmem, vmem),
        scratch_shapes=[pltpu.VMEM((BLK, BLK), jnp.float32)],
        compiler_params=pltpu.CompilerParams(vmem_limit_bytes=VMEM_LIMIT),
    )(place, partial, rest, *pieces)


def graft_step(sums_ref, update_ref, out_ref):
    totals = jnp.sum(sums_ref[...], axis=0)
    lane = lax.broadcasted_iota(jnp.int32, totals.shape, 1)
    grad_squares = jnp.sum(jnp.where(lane == 0, totals, 0.0))
    update_squares = jnp.sum(jnp.where(lane == 1, totals, 0.0))
    out_ref[...] = update_ref[...] * jnp.sqrt(grad_squares / update_squares)


def graft(sums, update):
    vmem = pl.BlockSpec(memory_space=pltpu.VMEM)
    return pl.pallas_call(
        graft_step,
        out_shape=jax.ShapeDtypeStruct(update.shape, update.dtype),
        in_specs=[vmem, vmem],
        out_specs=vmem,
        compiler_params=pltpu.CompilerParams(vmem_limit_bytes=GRAFT_LIMIT),
    )(sums, update)


def swap(value, axes, bits):
    size = 1
    for axis in axes:
        size *= lax.axis_size(axis)
    return lax.ppermute(value, axes, [(i, i ^ bits) for i in range(size)])


def swap_planes(value, up):
    step = 1 if up else -1
    pairs = [(i, (i + (step if i % 2 == 0 else -step)) % 8) for i in range(8)]
    return lax.ppermute(value, "prec", pairs)


def per_device(activations, output_grads, iter_counts):
    odd = lax.axis_index("prec") % 2
    place = jnp.stack([iter_counts[0, 0], lax.axis_index(DP), odd]).reshape(1, 3).astype(jnp.int32)
    own = activations.T
    near = [swap(own, ("x",), bits) for bits in (1, 3)]
    mine, here, *near_grads = cut(place, output_grads)
    three = jnp.stack([own] + near)
    mine, three = lax.optimization_barrier((mine, three))
    mine = lax.all_to_all(mine, DP, 0, 0, tiled=True)
    three_y = swap(three, ("yl", "pair"), 3)
    last = swap(three[1:2], ("x",), 3)
    far_three = [swap(value, ("core",), 1) for value in (three, three_y)]
    ready, _ = lax.optimization_barrier((mine, far_three))
    first, second = pick(place, ready)
    last, _ = lax.optimization_barrier((last, (first, second)))
    ways = (("x", 1), ("x", 3), ("yl", 1))
    near_grads, _ = lax.optimization_barrier((near_grads, (first, second)))
    near_grads = [swap(value, (axis,), bits) for value, (axis, bits) in zip(near_grads, ways, strict=True)]
    picked = first, second
    first, second = swap_planes(first, True), swap_planes(second, False)
    last_y = swap(last, ("yl", "pair"), 3)
    far_last = [swap(value, ("core",), 1) for value in (last, last_y)]
    acts = [three, three_y, *far_three]
    late = [last, last_y, *far_last]
    near_grads, _ = lax.optimization_barrier((near_grads, (first, second)))
    near_grads = [here] + near_grads
    partial, rest = half_gradient(place, mine, acts)
    leaving, _ = lax.optimization_barrier((jnp.stack([value[1] for value in near_grads]), partial))
    taken = swap(leaving, ("core",), 1)

    devices = 256
    update, sums = run_block(place, partial, rest, (*late, *picked, first, second, taken, *near_grads), devices)
    sums = lax.all_to_all(sums, EVERY, 0, 0, tiled=True)
    return graft(sums, update)


def solution(mesh):
    fine = Mesh(mesh.devices.reshape(4, 2, 2, 8, 2), EVERY)
    in_specs = (P(DP, "prec"), P(DP, "pair"), P(("pair",) + DP, "prec"))
    out_specs = P(("pair",) + DP, "prec")
    return jax.shard_map(
        per_device, mesh=fine, in_specs=in_specs, out_specs=out_specs, check_vma=False
    )
```
